32 devices in a mesh: node: 8 (over y, x, core), dev: 4 (over z).
Axes of the slice: x: 2, y: 2, z: 4, core: 2. Of those that a mesh axis runs over, the one named last changes fastest.
Arguments:
- tokens: bfloat16 [128, 4096], P('node', 'dev'), may hold values from -6 to 6
- routes: int32 [128, 8], P('node'), may hold values from 0 to 7, as said below
- gate_codes: int32 [128, 8], P('node'), may hold values from 1 to 65535
- w_gate: bfloat16 [8, 4096, 2048], P('node', None, 'dev'), may hold values from -0.09375 to 0.09375
- w_up: bfloat16 [8, 4096, 2048], P('node', None, 'dev'), may hold values from -0.09375 to 0.09375
- w_down: bfloat16 [8, 2048, 4096], P('node', 'dev'), may hold values from -0.125 to 0.125
- cotangent: bfloat16 [128, 4096], P('node', 'dev'), may hold values from -6 to 6
Outputs:
- layer_out: bfloat16 [128, 4096], P('node', 'dev')
- token_grad: bfloat16 [128, 4096], P('node', 'dev')
- down_grad: bfloat16 [8, 2048, 4096], P('node', 'dev')
The draws below stay inside these ranges and needn't reach their ends.
Inputs may be any that keep to these rules, and one draw needn't show every extreme that they name: `routes`: each token names 8 different experts, taken from at most 4 groups of 4 consecutive experts. Among the 16 tokens of one block (one index of node), no expert is named by more than 16 tokens, and in every block some expert is named by exactly 16.
All inputs are finite; a program needn't handle non-finite values.
Results may differ from the reference program's by a relative error of at most 0.012.
Values may be sent and summed in bfloat16 or wider, within the bound.
A program may use at most 64 MiB of HBM per device.

```python
import jax
import jax.numpy as jnp
from jax import lax

D = 4096
H = 2048
TOP = 8
TOP_GROUPS = 4
GROUP_SIZE = 4
TOK_NODE = 16
EXPERTS = 8
GROUPS = 2
CAP = 16
TOKENS = 128
HS = 512
N_DEV = 4


def draw_routes(key, part):
    block_count = TOKENS // TOK_NODE
    chosen_count = min(TOP_GROUPS, GROUPS)
    per_group = TOP // chosen_count

    def one_block(block_key):
        key_groups, key_tokens, key_hot, key_scores = jax.random.split(block_key, 4)
        group_order = jax.random.permutation(key_groups, GROUPS)
        token_order = jax.random.permutation(key_tokens, TOK_NODE)
        hot_slot = jax.random.randint(key_hot, (), 0, GROUP_SIZE)
        offsets = jnp.arange(TOK_NODE)[:, None] + jnp.arange(chosen_count)[None, :]
        chosen = group_order[offsets % GROUPS]
        scores = jax.random.randint(key_scores, (TOK_NODE, chosen_count, GROUP_SIZE), 0, 1024) * GROUP_SIZE + jnp.arange(GROUP_SIZE)[None, None, :]
        hot_pick = (chosen == group_order[0])[:, :, None] & (jnp.arange(GROUP_SIZE)[None, None, :] == hot_slot)
        scores = jnp.where(hot_pick, -1, scores)
        inside = jnp.argsort(scores, axis=2)[:, :, :per_group]
        experts_named = chosen[:, :, None] * GROUP_SIZE + inside
        flattened = experts_named.reshape(TOK_NODE, TOP)
        return flattened[token_order]
    block_keys = jax.random.split(key, block_count)
    return jax.vmap(one_block)(block_keys).reshape(TOKENS, TOP).astype(jnp.int32)


def with_ends(result, own_key, low, high):
    extent = result.shape
    place = [jax.random.randint(jax.random.fold_in(own_key, axis), (), 0, extent[axis]) for axis in range(len(extent))]
    result = result.at[tuple(place)].set(low)
    longest = extent.index(max(extent))
    place[longest] = (place[longest] + 1) % extent[longest]
    return result.at[tuple(place)].set(high)


def steps_of(own_key, extent, cuts, low, top_value):
    def one(dim, shards_of):
        heights = jax.random.uniform(jax.random.fold_in(jax.random.fold_in(own_key, 6), dim), (shards_of,), jnp.float32, low / len(cuts), top_value / len(cuts))
        return jnp.repeat(jnp.exp(heights), extent[dim] // shards_of).reshape((-1,) + (1,) * (len(extent) - dim - 1))

    gain = one(*cuts[0])
    for cut in cuts[1:]:
        gain = gain * one(*cut)
    return gain


def normal_values(own_key, dims, scale, reach, shards=(), held_as=jnp.bfloat16):
    level = steps_of(own_key, dims, shards, -0.22, 0.18) if shards else 1.0
    array = jax.random.normal(own_key, dims, jnp.float32) * scale * level
    return jnp.minimum(jnp.maximum(array, -reach), reach).astype(held_as)


def setup_inputs(seed: int = 0) -> dict:
    keys = jax.random.split(jax.random.key(seed), 8)
    return {
        "tokens": normal_values(keys[0], (TOKENS, D), 1.0, 6.0, ((0, 8), (1, 4))),
        "routes": draw_routes(jax.random.fold_in(keys[7], 71), 0),
        "gate_codes": with_ends(jax.random.randint(keys[2], (TOKENS, TOP), 1, 65536), jax.random.fold_in(keys[2], 1), 1, 65535).astype(jnp.int32),
        "w_gate": normal_values(keys[3], (EXPERTS, D, H), D ** -0.5, 0.09375, ((0, 8), (2, 4))),
        "w_up": normal_values(keys[4], (EXPERTS, D, H), D ** -0.5, 0.09375, ((0, 8), (2, 4))),
        "w_down": normal_values(keys[5], (EXPERTS, H, D), H ** -0.5, 0.125, ((0, 8), (1, 4))),
        "cotangent": normal_values(keys[6], (TOKENS, D), 1.0, 6.0, ((0, 8), (1, 4))),
    }


exact_mode = lax.Precision.HIGHEST


def slot_layout(routes, gate_codes, experts, capacity):
    tokens_here = routes.shape[0]
    member = (routes[:, :, None] == jnp.arange(experts, dtype=jnp.int32)[None, None, :]).astype(jnp.float32)
    named_by = jnp.sum(member, axis=1)
    earlier = (jnp.arange(tokens_here)[:, None] > jnp.arange(tokens_here)[None, :]).astype(jnp.float32)
    before = jnp.dot(earlier, named_by, precision=exact_mode)
    placed = named_by[:, :, None] * (before[:, :, None] == jnp.arange(capacity).astype(jnp.float32)[None, None, :]).astype(jnp.float32)
    weights = gate_codes.astype(jnp.float32) / 65536.0
    gating = jnp.sum(member * weights[:, :, None], axis=1)
    return placed, gating


def block_layout(route_block, code_block):
    return slot_layout(route_block, code_block, EXPERTS, CAP)


def rounded_sum(parts):
    return jnp.sum(lax.optimization_barrier(parts.astype(jnp.bfloat16)).astype(jnp.float32), axis=0)


def reference(tokens, routes, gate_codes, w_gate, w_up, w_down, cotangent):
    placed, gating = jax.vmap(block_layout)(routes.reshape(EXPERTS, TOK_NODE, TOP), gate_codes.reshape(EXPERTS, TOK_NODE, TOP))
    weighted = placed * gating[:, :, :, None]
    token_blocks = tokens.reshape(EXPERTS, TOK_NODE, D).astype(jnp.float32)
    cot_blocks = cotangent.reshape(EXPERTS, TOK_NODE, D).astype(jnp.float32)
    slots_all = EXPERTS * CAP

    def per_expert(operands):
        place_e, weight_e, gate_mat, up_mat, down_mat = operands
        rows_in = jnp.einsum("btp,btf->bpf", place_e, token_blocks, precision=exact_mode).astype(jnp.bfloat16).reshape(slots_all, D)
        gate_pre = jnp.dot(rows_in, gate_mat, preferred_element_type=jnp.float32)
        up_pre = jnp.dot(rows_in, up_mat, preferred_element_type=jnp.float32)
        squash = jax.nn.sigmoid(gate_pre)
        hidden = (gate_pre * squash * up_pre).astype(jnp.bfloat16)
        hid_blocks = hidden.astype(jnp.float32).reshape(slots_all, N_DEV, HS)
        out_parts = jnp.einsum("rsh,shf->srf", hid_blocks, down_mat.astype(jnp.float32).reshape(N_DEV, HS, D), precision=exact_mode)
        expert_rows = rounded_sum(out_parts).astype(jnp.bfloat16)
        weighted_cot = jnp.einsum("btp,btf->bpf", weight_e, cot_blocks, precision=exact_mode).astype(jnp.bfloat16).reshape(slots_all, D)
        hidden_grad = jnp.dot(weighted_cot, down_mat.T, preferred_element_type=jnp.float32)
        down_grad = jnp.dot(hidden.T, weighted_cot, preferred_element_type=jnp.float32).astype(jnp.bfloat16)
        gate_grad = (hidden_grad * up_pre * squash * (1.0 + gate_pre * (1.0 - squash))).astype(jnp.bfloat16)
        up_grad = (hidden_grad * gate_pre * squash).astype(jnp.bfloat16)
        gate_blocks = gate_grad.astype(jnp.float32).reshape(slots_all, N_DEV, HS)
        up_blocks = up_grad.astype(jnp.float32).reshape(slots_all, N_DEV, HS)
        back_parts = jnp.einsum("rsh,fsh->srf", gate_blocks, gate_mat.astype(jnp.float32).reshape(D, N_DEV, HS), precision=exact_mode)
        back_parts = back_parts + jnp.einsum("rsh,fsh->srf", up_blocks, up_mat.astype(jnp.float32).reshape(D, N_DEV, HS), precision=exact_mode)
        back_rows = rounded_sum(back_parts).astype(jnp.bfloat16)
        return expert_rows.reshape(EXPERTS, CAP, D), back_rows.reshape(EXPERTS, CAP, D), down_grad

    place_by_expert = jnp.transpose(placed, (2, 0, 1, 3))
    weight_by_expert = jnp.transpose(weighted, (2, 0, 1, 3))
    expert_rows, back_rows, down_grad = lax.map(per_expert, (place_by_expert, weight_by_expert, w_gate, w_up, w_down))
    layer_out = jnp.einsum("btep,ebpf->btf", weighted, expert_rows.astype(jnp.float32), precision=exact_mode)
    token_grad = jnp.einsum("btep,ebpf->btf", placed, back_rows.astype(jnp.float32), precision=exact_mode)
    return (layer_out.reshape(TOKENS, D).astype(jnp.bfloat16), token_grad.reshape(TOKENS, D).astype(jnp.bfloat16), down_grad)
```

```python
import jax
import jax.numpy as jnp
from jax import lax
from jax.experimental import pallas as pl
from jax.experimental.pallas import tpu as pltpu
from jax.sharding import PartitionSpec as P

TOP_GROUPS = 4
GROUP_SIZE = 4
MESH_IDS = pl.DeviceIdType.MESH
ORDER_IN = (0, 1, 3, 2)
ORDER_OUT = (2, 1, 3, 0)


def dot(a, b, a_dim=1, b_dim=0):
    return lax.dot_general(
        a, b, (((a_dim,), (b_dim,)), ((), ())), preferred_element_type=jnp.float32
    )


def fused_kernel(
    tok_in, routes_in, codes_in, wg_in, wu_in, wd_in, cot_in,
    layer_out, token_grad, down_out,
    x_all, gates, wg, wu, wd, gate_pre, up_pre, hid_grad, hidden, wcot, gate_grad, up_grad,
    part, r1, s1, r2, s2, r3, s3, r4, dgrad,
    in_send, in_recv, g_send, g_recv, out_send, out_recv, w_sem, own_sem, d_sem,
):
    node, d = lax.axis_index("node"), lax.axis_index("dev")
    y, x, c = node // 4, (node // 2) % 2, node % 2
    x_peer = (y * 2 + 1 - x) * 2 + c
    y_peer = ((1 - y) * 2 + x) * 2 + c
    c_peer = (y * 2 + x) * 2 + 1 - c
    width = tok_in.shape[1]
    rows = 8 * tok_in.shape[0]
    sent = []

    def send(src, dst, send_sem, recv_sem, target):
        copy = pltpu.make_async_remote_copy(
            src_ref=src, dst_ref=dst, send_sem=send_sem, recv_sem=recv_sem,
            device_id=target, device_id_type=MESH_IDS,
        )
        copy.start()
        sent.append(copy)
        return copy

    def column(k):
        return pl.ds(pl.multiple_of(((d + k) % 4) * width, width), width)

    barrier = pltpu.get_barrier_semaphore()
    peers = [(x_peer, d), (y_peer, d), (c_peer, d)] + [(node, (d + j) % 4) for j in (1, 2, 3)]
    for peer in peers:
        pl.semaphore_signal(barrier, inc=1, device_id=peer, device_id_type=MESH_IDS)

    loads = {}
    for k in ORDER_IN:
        loads["g", k] = pltpu.make_async_copy(wg_in.at[0, column(k)], wg.at[k], w_sem.at[0, k])
        loads["u", k] = pltpu.make_async_copy(wu_in.at[0, column(k)], wu.at[k], w_sem.at[1, k])
    for k in range(4):
        loads["d", k] = pltpu.make_async_copy(
            wd_in.at[0, :, column(k)], wd.at[k], w_sem.at[2, k]
        )
    for load in loads.values():
        load.start()

    lane = lax.broadcasted_iota(jnp.int32, (tok_in.shape[0], 128), 1)
    table = jnp.zeros((tok_in.shape[0], 128), jnp.float32)
    for j in range(routes_in.shape[1]):
        table = table + jnp.where(
            routes_in[:, j : j + 1] == lane,
            codes_in[:, j : j + 1].astype(jnp.float32) / 65536.0,
            0.0,
        )
    gates[y, x, c] = table
    x_all[0, 0, y, x, c] = tok_in[...]
    x_all[1, 0, y, x, c] = cot_in[...]

    pl.semaphore_wait(barrier, 6)

    z_hop = {}

    def start_z(a):
        own = tok_in if a == 0 else cot_in
        for j in (1, 3, 2):
            z_hop[a, 4 - j] = send(
                own, x_all.at[a, 4 - j, y, x, c], in_send.at[a, j, 0], in_recv.at[a, 4 - j, 0],
                (node, (d + j) % 4),
            )

    hop = {}

    def gather_stage(block, stage):
        a, i = divmod(block, 4)
        k = ORDER_IN[i]
        x_first = i % 2 == 0
        if stage == 0:
            if k:
                z_hop[a, k].wait_recv()
            ref = x_all.at[a, k, y, x, c]
            target = x_peer if x_first else y_peer
        else:
            hop[a, k].wait_recv()
            if stage == 1 and x_first:
                ref, target = x_all.at[a, k, y, :, c], y_peer
            elif stage == 1:
                ref, target = x_all.at[a, k, :, x, c], x_peer
            elif stage == 2:
                ref, target = x_all.at[a, k, :, :, c], c_peer
            else:
                return
        hop[a, k] = send(
            ref, ref, in_send.at[a, k, stage + 1], in_recv.at[a, k, stage + 1], (target, d)
        )

    def gates_stage(stage):
        if stage:
            hop["gates"].wait_recv()
        if stage < 3:
            ref, target = (
                (gates.at[y, x, c], x_peer),
                (gates.at[y, :, c], y_peer),
                (gates.at[:, :, c], c_peer),
            )[stage]
            hop["gates"] = send(ref, ref, g_send.at[stage], g_recv.at[stage], (target, d))

    def own_gates():
        table = gates[...].reshape(rows, 128)
        mine = lax.broadcasted_iota(jnp.int32, (rows, 128), 1) == node
        return jnp.sum(jnp.where(mine, table, 0.0), axis=1, keepdims=True)

    def project_in(i):
        k = ORDER_IN[i]
        lhs = x_all[0, k].reshape(rows, width)
        for name, weight, total in (("g", wg, gate_pre), ("u", wu, up_pre)):
            loads[name, k].wait()
            product = dot(lhs, weight[k])
            if i == 0:
                total[...] = product
            else:
                total[...] += product

    def make_hidden():
        pre = gate_pre[...]
        hidden[...] = (pre * jax.nn.sigmoid(pre) * up_pre[...]).astype(jnp.bfloat16)
        for k in range(4):
            loads["d", k].wait()

    def project_cotangent(i):
        k = ORDER_IN[i]
        values = x_all[1, k].reshape(rows, width).astype(jnp.float32)
        wcot[k] = (own_gates() * values).astype(jnp.bfloat16)
        product = dot(wcot[k], wd[k], 1, 1)
        if i == 0:
            hid_grad[...] = product
        else:
            hid_grad[...] += product

    def make_grads():
        pre, grad = gate_pre[...], hid_grad[...]
        q = jax.nn.sigmoid(pre)
        gate_grad[...] = (grad * up_pre[...] * q * (1.0 + pre * (1.0 - q))).astype(jnp.bfloat16)
        up_grad[...] = (grad * pre * q).astype(jnp.bfloat16)

    back = {}

    def add(one, other):
        return (one.astype(jnp.float32) + other.astype(jnp.float32)).astype(jnp.bfloat16)

    def return_stage(block, stage):
        b, i = divmod(block, 4)
        k = ORDER_OUT[i]
        x_first = i % 2 == 0
        if stage == 0:
            if b == 0:
                value = own_gates() * dot(hidden[...], wd[k])
            else:
                value = dot(gate_grad[...], wg[k], 1, 1) + dot(up_grad[...], wu[k], 1, 1)
            part[b, k] = value.astype(jnp.bfloat16).reshape(part.shape[2:])
            src, dst, target = part.at[b, k, :, :, 1 - c], r1.at[b, k], c_peer
        elif stage == 1:
            back[b, k].wait_recv()
            s1[b, k] = add(part[b, k, :, :, c], r1[b, k])
            if x_first:
                src, target = s1.at[b, k, :, 1 - x], x_peer
            else:
                src, target = s1.at[b, k, 1 - y], y_peer
            dst = r2.at[b, k]
        elif stage == 2:
            back[b, k].wait_recv()
            s2[b, k] = add(s1[b, k, :, x] if x_first else s1[b, k, y], r2[b, k])
            if x_first:
                src, target = s2.at[b, k, 1 - y], y_peer
            else:
                src, target = s2.at[b, k, 1 - x], x_peer
            dst = r3.at[b, k]
        else:
            back[b, k].wait_recv()
            s3[b, k] = add(s2[b, k, y] if x_first else s2[b, k, x], r3[b, k])
            if k:
                back[b, "z", 4 - k] = send(
                    s3.at[b, k], r4.at[b, 4 - k], out_send.at[b, k, 3], out_recv.at[b, 4 - k, 3],
                    (node, (d + k) % 4),
                )
            return
        back[b, k] = send(
            src, dst, out_send.at[b, k, stage], out_recv.at[b, k, stage], (target, d)
        )

    def finish(b, result):
        total = s3[b, 0].astype(jnp.float32)
        for k in (1, 3, 2):
            back[b, "z", k].wait_recv()
            total = total + r4[b, k].astype(jnp.float32)
        result[...] = total.astype(jnp.bfloat16)

    stores = []

    def down_block(k):
        dgrad[k] = dot(hidden[...], wcot[k], 0, 0).astype(jnp.bfloat16)
        store = pltpu.make_async_copy(dgrad.at[k], down_out.at[0, :, column(k)], d_sem.at[k])
        store.start()
        stores.append(store)

    start_z(0)
    gates_stage(0)
    for slot in range(18):
        for stage in (3, 2, 1, 0):
            if 0 <= slot - stage < 8:
                gather_stage(slot - stage, stage)
        if slot == 0:
            start_z(1)
        if 1 <= slot <= 3:
            gates_stage(slot)
        for stage in (3, 2, 1):
            if 0 <= slot - 7 - stage < 8:
                return_stage(slot - 7 - stage, stage)
        if 3 <= slot <= 6:
            project_in(slot - 3)
        if slot == 6:
            make_hidden()
        if 7 <= slot <= 14:
            return_stage(slot - 7, 0)
        if 7 <= slot <= 10:
            project_cotangent(slot - 7)
        if slot == 10:
            make_grads()
        if slot >= 14:
            down_block(slot - 14)
        if slot == 15:
            finish(0, layer_out)
    finish(1, token_grad)
    for copy in sent:
        copy.wait_send()
    for store in stores:
        store.wait()


def fused(tokens, routes, gate_codes, w_gate, w_up, w_down, cotangent):
    here, width = tokens.shape
    hidden_width = w_gate.shape[2]
    rows = 8 * here
    low, full = jnp.bfloat16, jnp.float32
    vmem = pl.BlockSpec(memory_space=pltpu.VMEM)
    anywhere = pl.BlockSpec(memory_space=pl.ANY)
    dma = pltpu.SemaphoreType.DMA
    scratch = [
        pltpu.VMEM((2, 4, 2, 2, 2, here, width), low),
        pltpu.VMEM((2, 2, 2, here, 128), full),
        pltpu.VMEM((4, width, hidden_width), low),
        pltpu.VMEM((4, width, hidden_width), low),
        pltpu.VMEM((4, hidden_width, width), low),
        pltpu.VMEM((rows, hidden_width), full),
        pltpu.VMEM((rows, hidden_width), full),
        pltpu.VMEM((rows, hidden_width), full),
        pltpu.VMEM((rows, hidden_width), low),
        pltpu.VMEM((4, rows, width), low),
        pltpu.VMEM((rows, hidden_width), low),
        pltpu.VMEM((rows, hidden_width), low),
        pltpu.VMEM((2, 4, 2, 2, 2, here, width), low),
        pltpu.VMEM((2, 4, 2, 2, here, width), low),
        pltpu.VMEM((2, 4, 2, 2, here, width), low),
        pltpu.VMEM((2, 4, 2, here, width), low),
        pltpu.VMEM((2, 4, 2, here, width), low),
        pltpu.VMEM((2, 4, here, width), low),
        pltpu.VMEM((2, 4, here, width), low),
        pltpu.VMEM((2, 4, here, width), low),
        pltpu.VMEM((4, hidden_width, width), low),
        dma((2, 4, 4)), dma((2, 4, 4)), dma((3,)), dma((3,)), dma((2, 4, 4)), dma((2, 4, 4)),
        dma((3, 4)), dma((2,)), dma((4,)),
    ]
    flops = 2 * 7 * rows * 4 * width * hidden_width
    return pl.pallas_call(
        fused_kernel,
        out_shape=(
            jax.ShapeDtypeStruct(tokens.shape, low),
            jax.ShapeDtypeStruct(tokens.shape, low),
            jax.ShapeDtypeStruct(w_down.shape, low),
        ),
        in_specs=[vmem, vmem, vmem, anywhere, anywhere, anywhere, vmem],
        out_specs=(vmem, vmem, anywhere),
        scratch_shapes=scratch,
        compiler_params=pltpu.CompilerParams(
            collective_id=0, has_side_effects=True, vmem_limit_bytes=48 * 1024 * 1024
        ),
        cost_estimate=pl.CostEstimate(
            flops=flops, bytes_accessed=8 * w_gate.size, transcendentals=2 * rows * hidden_width
        ),
    )(tokens, routes, gate_codes, w_gate, w_up, w_down, cotangent)


exact_mode = lax.Precision.HIGHEST


def slot_layout(routes, gate_codes, experts, capacity):
    tokens_here = routes.shape[0]
    member = (routes[:, :, None] == jnp.arange(experts, dtype=jnp.int32)[None, None, :]).astype(
        jnp.float32
    )
    named_by = jnp.sum(member, axis=1)
    earlier = (jnp.arange(tokens_here)[:, None] > jnp.arange(tokens_here)[None, :]).astype(
        jnp.float32
    )
    before = jnp.dot(earlier, named_by, precision=exact_mode)
    placed = named_by[:, :, None] * (
        before[:, :, None] == jnp.arange(capacity).astype(jnp.float32)[None, None, :]
    ).astype(jnp.float32)
    weights = gate_codes.astype(jnp.float32) / 65536.0
    gating = jnp.sum(member * weights[:, :, None], axis=1)
    return (placed, gating)


def deliver(local_rows, build, fold, initial):
    whole_rows = lax.all_gather(local_rows, "dev", axis=1, tiled=True)
    arrived = lax.all_to_all(build(whole_rows), "node", split_axis=0, concat_axis=0, tiled=True)
    return fold(initial, arrived, 0)


def send_back(partial_value):
    shares = lax.psum_scatter(
        partial_value.astype(jnp.bfloat16), "dev", scatter_dimension=2, tiled=True
    )
    return lax.all_to_all(shares, "node", split_axis=0, concat_axis=0, tiled=True)


def on_device(tokens, routes, gate_codes, w_gate, w_up, w_down, cotangent):
    experts = lax.axis_size("node")
    groups = experts // GROUP_SIZE
    chosen_count = min(TOP_GROUPS, groups)
    capacity = tokens.shape[0] * chosen_count // groups
    placed, gating = slot_layout(routes, gate_codes, experts, capacity)
    place_low = placed.astype(jnp.bfloat16)
    weighted = placed * gating[:, :, None]
    gate_mat = w_gate[0]
    up_mat = w_up[0]
    down_mat = w_down[0]
    hidden_width = gate_mat.shape[1]

    def spread_tokens(payload):
        return jnp.einsum(
            "tep,tf->epf", place_low, payload, preferred_element_type=jnp.float32
        ).astype(jnp.bfloat16)

    def spread_cotangent(payload):
        return jnp.einsum(
            "tep,tf->epf", weighted, payload.astype(jnp.float32), precision=exact_mode
        ).astype(jnp.bfloat16)

    def project_in(totals, portion, offset):
        gate_next = jnp.einsum("epf,fh->eph", portion, gate_mat, preferred_element_type=jnp.float32)
        up_next = jnp.einsum("epf,fh->eph", portion, up_mat, preferred_element_type=jnp.float32)
        return (gate_next, up_next)

    empty_hidden = jnp.zeros((experts, capacity, hidden_width), jnp.float32)
    gate_pre, up_pre = deliver(tokens, spread_tokens, project_in, (empty_hidden, empty_hidden))
    squash = jax.nn.sigmoid(gate_pre)
    hidden = (gate_pre * squash * up_pre).astype(jnp.bfloat16)
    partial_value = jnp.einsum("eph,hf->epf", hidden, down_mat, preferred_element_type=jnp.float32)
    returned = send_back(partial_value)
    layer_out = jnp.einsum(
        "tep,epf->tf", weighted, returned.astype(jnp.float32), precision=exact_mode
    ).astype(jnp.bfloat16)

    def project_cotangent(totals, portion, offset):
        grad_next = jnp.einsum("epf,hf->eph", portion, down_mat, preferred_element_type=jnp.float32)
        block_grad = jnp.einsum("eph,epf->hf", hidden, portion, preferred_element_type=jnp.float32)
        return (grad_next, block_grad)

    empty_down = jnp.zeros((hidden_width, down_mat.shape[1]), jnp.float32)
    hidden_grad, down_total = deliver(
        cotangent, spread_cotangent, project_cotangent, (empty_hidden, empty_down)
    )
    gate_grad = (hidden_grad * up_pre * squash * (1.0 + gate_pre * (1.0 - squash))).astype(
        jnp.bfloat16
    )
    up_grad = (hidden_grad * gate_pre * squash).astype(jnp.bfloat16)
    partial_back = jnp.einsum(
        "eph,fh->epf", gate_grad, gate_mat, preferred_element_type=jnp.float32
    )
    partial_back = partial_back + jnp.einsum(
        "eph,fh->epf", up_grad, up_mat, preferred_element_type=jnp.float32
    )
    returned_back = send_back(partial_back)
    token_grad = jnp.einsum(
        "tep,epf->tf", placed, returned_back.astype(jnp.float32), precision=exact_mode
    ).astype(jnp.bfloat16)
    return (layer_out, token_grad, down_total.astype(jnp.bfloat16)[None])


def solution(mesh):
    in_specs = (
        P("node", "dev"),
        P("node", None),
        P("node", None),
        P("node", None, "dev"),
        P("node", None, "dev"),
        P("node", "dev", None),
        P("node", "dev"),
    )
    out_specs = (P("node", "dev"), P("node", "dev"), P("node", "dev", None))
    nodes, devs = mesh.shape["node"], mesh.shape["dev"]

    def body(tokens, routes, *rest):
        every = routes.shape[1] == nodes
        layer = fused if every and nodes == 8 and devs == 4 else on_device
        return layer(tokens, routes, *rest)

    return jax.shard_map(
        body, mesh=mesh, in_specs=in_specs, out_specs=out_specs, check_vma=False
    )
```

```python
import jax
import jax.numpy as jnp
from jax import lax
from jax.experimental import pallas as pl
from jax.experimental.pallas import tpu as pltpu
from jax.sharding import PartitionSpec as P

TOP_GROUPS = 4
GROUP_SIZE = 4
MESH_IDS = pl.DeviceIdType.MESH
ORDER_IN = (0, 1, 3, 2)
ORDER_OUT = (2, 1, 3, 0)
GROUP = 2


def dot(a, b, a_dim=1, b_dim=0):
    return lax.dot_general(
        a, b, (((a_dim,), (b_dim,)), ((), ())), preferred_element_type=jnp.float32
    )


def fused_kernel(
    tok_in, routes_in, codes_in, wg_in, wu_in, wd_in, cot_in,
    layer_out, token_grad, down_out,
    x_all, gates, wg, wu, wd, gate_pre, up_pre, hid_grad, hidden, wcot, gate_grad, up_grad,
    part, r1, s1, r2, s2, r3, s3, r4, dgrad,
    in_send, in_recv, g_send, g_recv, out_send, out_recv, w_sem, own_sem, d_sem, named, codes,
):
    node, d = lax.axis_index("node"), lax.axis_index("dev")
    y, x, c = node // 4, (node // 2) % 2, node % 2
    x_peer = (y * 2 + 1 - x) * 2 + c
    y_peer = ((1 - y) * 2 + x) * 2 + c
    c_peer = (y * 2 + x) * 2 + 1 - c
    width = tok_in.shape[1]
    rows = 8 * tok_in.shape[0]
    sent = []

    def send(src, dst, send_sem, recv_sem, target):
        copy = pltpu.make_async_remote_copy(
            src_ref=src, dst_ref=dst, send_sem=send_sem, recv_sem=recv_sem,
            device_id=target, device_id_type=MESH_IDS,
        )
        copy.start()
        sent.append(copy)
        return copy

    def column(k):
        return pl.ds(pl.multiple_of(((d + k) % 4) * width, width), width)

    barrier = pltpu.get_barrier_semaphore()
    peers = [(x_peer, d), (y_peer, d), (c_peer, d)] + [(node, (d + j) % 4) for j in (1, 2, 3)]
    for peer in peers:
        pl.semaphore_signal(barrier, inc=1, device_id=peer, device_id_type=MESH_IDS)

    own = [
        pltpu.make_async_copy(src, dst, own_sem.at[n])
        for n, (src, dst) in enumerate((
            (tok_in, x_all.at[0, 0, y, x, c]), (cot_in, x_all.at[1, 0, y, x, c]),
            (routes_in, named), (codes_in, codes),
        ))
    ]
    for copy in own:
        copy.start()

    loads = {}
    for k in ORDER_IN:
        loads["g", k] = pltpu.make_async_copy(wg_in.at[0, column(k)], wg.at[k], w_sem.at[0, k])
        loads["u", k] = pltpu.make_async_copy(wu_in.at[0, column(k)], wu.at[k], w_sem.at[1, k])
    for k in range(4):
        loads["d", k] = pltpu.make_async_copy(
            wd_in.at[0, :, column(k)], wd.at[k], w_sem.at[2, k]
        )
    for load in loads.values():
        load.start()

    for copy in own:
        copy.wait()
    lane = lax.broadcasted_iota(jnp.int32, (tok_in.shape[0], 128), 1)
    table = jnp.zeros((tok_in.shape[0], 128), jnp.float32)
    for j in range(routes_in.shape[1]):
        table = table + jnp.where(
            named[:, j : j + 1] == lane,
            codes[:, j : j + 1].astype(jnp.float32) / 65536.0,
            0.0,
        )
    gates[y, x, c] = table

    pl.semaphore_wait(barrier, 6)

    z_hop = {}

    def start_z(a):
        own = x_all.at[a, 0, y, x, c]
        for j in (1, 3, 2):
            z_hop[a, 4 - j] = send(
                own, x_all.at[a, 4 - j, y, x, c], in_send.at[a, j, 0], in_recv.at[a, 4 - j, 0],
                (node, (d + j) % 4),
            )

    hop = {}

    def gather_stage(block, stage):
        a, i = divmod(block, 4)
        k = ORDER_IN[i]
        x_first = i % 2 == 0
        if stage == 0:
            if k:
                z_hop[a, k].wait_recv()
            ref = x_all.at[a, k, y, x, c]
            target = x_peer if x_first else y_peer
        else:
            hop[a, k].wait_recv()
            if stage == 1 and x_first:
                ref, target = x_all.at[a, k, y, :, c], y_peer
            elif stage == 1:
                ref, target = x_all.at[a, k, :, x, c], x_peer
            elif stage == 2:
                ref, target = x_all.at[a, k, :, :, c], c_peer
            else:
                return
        hop[a, k] = send(
            ref, ref, in_send.at[a, k, stage + 1], in_recv.at[a, k, stage + 1], (target, d)
        )

    def gates_stage(stage):
        if stage:
            hop["gates"].wait_recv()
        if stage < 3:
            ref, target = (
                (gates.at[y, x, c], x_peer),
                (gates.at[y, :, c], y_peer),
                (gates.at[:, :, c], c_peer),
            )[stage]
            hop["gates"] = send(ref, ref, g_send.at[stage], g_recv.at[stage], (target, d))

    def own_gates():
        table = gates[...].reshape(rows, 128)
        mine = lax.broadcasted_iota(jnp.int32, (rows, 128), 1) == node
        return jnp.sum(jnp.where(mine, table, 0.0), axis=1, keepdims=True)

    def project_in(i):
        k = ORDER_IN[i]
        lhs = x_all[0, k].reshape(rows, width)
        for name, weight, total in (("g", wg, gate_pre), ("u", wu, up_pre)):
            loads[name, k].wait()
            product = dot(lhs, weight[k])
            if i == 0:
                total[...] = product
            else:
                total[...] += product

    def make_hidden():
        pre = gate_pre[...]
        hidden[...] = (pre * jax.nn.sigmoid(pre) * up_pre[...]).astype(jnp.bfloat16)
        for k in range(4):
            loads["d", k].wait()

    def project_cotangent(i):
        k = ORDER_IN[i]
        values = x_all[1, k].reshape(rows, width).astype(jnp.float32)
        wcot[k] = (own_gates() * values).astype(jnp.bfloat16)
        product = dot(wcot[k], wd[k], 1, 1)
        if i == 0:
            hid_grad[...] = product
        else:
            hid_grad[...] += product

    def make_grads():
        pre, grad = gate_pre[...], hid_grad[...]
        q = jax.nn.sigmoid(pre)
        gate_grad[...] = (grad * up_pre[...] * q * (1.0 + pre * (1.0 - q))).astype(jnp.bfloat16)
        up_grad[...] = (grad * pre * q).astype(jnp.bfloat16)

    back = {}

    def add(one, other):
        return (one.astype(jnp.float32) + other.astype(jnp.float32)).astype(jnp.bfloat16)

    def return_stage(block, stage):
        b, i = divmod(block, 4)
        k = ORDER_OUT[i]
        x_first = i % 2 == 0
        if stage == 0:
            if b == 0:
                value = own_gates() * dot(hidden[...], wd[k])
            else:
                value = dot(gate_grad[...], wg[k], 1, 1) + dot(up_grad[...], wu[k], 1, 1)
            part[b, k] = value.astype(jnp.bfloat16).reshape(part.shape[2:])
            src, dst, target = part.at[b, k, :, :, 1 - c], r1.at[b, k], c_peer
        elif stage == 1:
            back[b, k].wait_recv()
            s1[b, k] = add(part[b, k, :, :, c], r1[b, k])
            if x_first:
                src, target = s1.at[b, k, :, 1 - x], x_peer
            else:
                src, target = s1.at[b, k, 1 - y], y_peer
            dst = r2.at[b, k]
        elif stage == 2:
            back[b, k].wait_recv()
            s2[b, k] = add(s1[b, k, :, x] if x_first else s1[b, k, y], r2[b, k])
            if x_first:
                src, target = s2.at[b, k, 1 - y], y_peer
            else:
                src, target = s2.at[b, k, 1 - x], x_peer
            dst = r3.at[b, k]
        else:
            back[b, k].wait_recv()
            s3[b, k] = add(s2[b, k, y] if x_first else s2[b, k, x], r3[b, k])
            if k:
                back[b, "z", 4 - k] = send(
                    s3.at[b, k], r4.at[b, 4 - k], out_send.at[b, k, 3], out_recv.at[b, 4 - k, 3],
                    (node, (d + k) % 4),
                )
            return
        back[b, k] = send(
            src, dst, out_send.at[b, k, stage], out_recv.at[b, k, stage], (target, d)
        )

    def finish(b, result):
        total = s3[b, 0].astype(jnp.float32)
        for k in (1, 3, 2):
            back[b, "z", k].wait_recv()
            total = total + r4[b, k].astype(jnp.float32)
        result[...] = total.astype(jnp.bfloat16)

    stores = []

    def down_block(k):
        dgrad[k] = dot(hidden[...], wcot[k], 0, 0).astype(jnp.bfloat16)
        store = pltpu.make_async_copy(dgrad.at[k], down_out.at[0, :, column(k)], d_sem.at[k])
        store.start()
        stores.append(store)

    start_z(0)
    gates_stage(0)
    groups = 8 // GROUP
    ready = groups // 2 + 2
    last = ready + groups + 3

    def members(group):
        return range(group * GROUP, group * GROUP + GROUP) if 0 <= group < groups else ()

    for slot in range(last):
        for stage in (3, 2, 1, 0):
            for block in members(slot - stage):
                gather_stage(block, stage)
        if slot == 0:
            start_z(1)
        if 1 <= slot <= 3:
            gates_stage(slot)
        for block in members(slot - 3):
            if block < 4:
                project_in(block)
        if slot == ready:
            make_hidden()
        for block in members(slot - ready):
            if block < 4:
                return_stage(block, 0)
        for block in members(slot - 3):
            if block >= 4:
                project_cotangent(block - 4)
        if slot == groups + 2:
            make_grads()
        for block in members(slot - ready):
            if block >= 4:
                return_stage(block, 0)
        if slot >= last - 3:
            for k in ((0, 1), (2,), (3,))[slot - (last - 3)]:
                down_block(k)
        for stage in (3, 2, 1):
            for block in members(slot - ready - stage):
                return_stage(block, stage)
    finish(0, layer_out)
    finish(1, token_grad)
    for copy in sent:
        copy.wait_send()
    for store in stores:
        store.wait()


def fused(tokens, routes, gate_codes, w_gate, w_up, w_down, cotangent):
    here, width = tokens.shape
    hidden_width = w_gate.shape[2]
    rows = 8 * here
    low, full = jnp.bfloat16, jnp.float32
    vmem = pl.BlockSpec(memory_space=pltpu.VMEM)
    anywhere = pl.BlockSpec(memory_space=pl.ANY)
    dma = pltpu.SemaphoreType.DMA
    scratch = [
        pltpu.VMEM((2, 4, 2, 2, 2, here, width), low),
        pltpu.VMEM((2, 2, 2, here, 128), full),
        pltpu.VMEM((4, width, hidden_width), low),
        pltpu.VMEM((4, width, hidden_width), low),
        pltpu.VMEM((4, hidden_width, width), low),
        pltpu.VMEM((rows, hidden_width), full),
        pltpu.VMEM((rows, hidden_width), full),
        pltpu.VMEM((rows, hidden_width), full),
        pltpu.VMEM((rows, hidden_width), low),
        pltpu.VMEM((4, rows, width), low),
        pltpu.VMEM((rows, hidden_width), low),
        pltpu.VMEM((rows, hidden_width), low),
        pltpu.VMEM((2, 4, 2, 2, 2, here, width), low),
        pltpu.VMEM((2, 4, 2, 2, here, width), low),
        pltpu.VMEM((2, 4, 2, 2, here, width), low),
        pltpu.VMEM((2, 4, 2, here, width), low),
        pltpu.VMEM((2, 4, 2, here, width), low),
        pltpu.VMEM((2, 4, here, width), low),
        pltpu.VMEM((2, 4, here, width), low),
        pltpu.VMEM((2, 4, here, width), low),
        pltpu.VMEM((4, hidden_width, width), low),
        dma((2, 4, 4)), dma((2, 4, 4)), dma((3,)), dma((3,)), dma((2, 4, 4)), dma((2, 4, 4)),
        dma((3, 4)), dma((4,)), dma((4,)),
        pltpu.VMEM(routes.shape, jnp.int32), pltpu.VMEM(gate_codes.shape, jnp.int32),
    ]
    flops = 2 * 7 * rows * 4 * width * hidden_width
    return pl.pallas_call(
        fused_kernel,
        out_shape=(
            jax.ShapeDtypeStruct(tokens.shape, low),
            jax.ShapeDtypeStruct(tokens.shape, low),
            jax.ShapeDtypeStruct(w_down.shape, low),
        ),
        in_specs=[anywhere] * 7,
        out_specs=(vmem, vmem, anywhere),
        scratch_shapes=scratch,
        compiler_params=pltpu.CompilerParams(
            collective_id=0, has_side_effects=True, vmem_limit_bytes=48 * 1024 * 1024
        ),
        cost_estimate=pl.CostEstimate(
            flops=flops, bytes_accessed=8 * w_gate.size, transcendentals=2 * rows * hidden_width
        ),
    )(tokens, routes, gate_codes, w_gate, w_up, w_down, cotangent)


exact_mode = lax.Precision.HIGHEST


def slot_layout(routes, gate_codes, experts, capacity):
    tokens_here = routes.shape[0]
    member = (routes[:, :, None] == jnp.arange(experts, dtype=jnp.int32)[None, None, :]).astype(
        jnp.float32
    )
    named_by = jnp.sum(member, axis=1)
    earlier = (jnp.arange(tokens_here)[:, None] > jnp.arange(tokens_here)[None, :]).astype(
        jnp.float32
    )
    before = jnp.dot(earlier, named_by, precision=exact_mode)
    placed = named_by[:, :, None] * (
        before[:, :, None] == jnp.arange(capacity).astype(jnp.float32)[None, None, :]
    ).astype(jnp.float32)
    weights = gate_codes.astype(jnp.float32) / 65536.0
    gating = jnp.sum(member * weights[:, :, None], axis=1)
    return (placed, gating)


def deliver(local_rows, build, fold, initial):
    whole_rows = lax.all_gather(local_rows, "dev", axis=1, tiled=True)
    arrived = lax.all_to_all(build(whole_rows), "node", split_axis=0, concat_axis=0, tiled=True)
    return fold(initial, arrived, 0)


def send_back(partial_value):
    shares = lax.psum_scatter(
        partial_value.astype(jnp.bfloat16), "dev", scatter_dimension=2, tiled=True
    )
    return lax.all_to_all(shares, "node", split_axis=0, concat_axis=0, tiled=True)


def on_device(tokens, routes, gate_codes, w_gate, w_up, w_down, cotangent):
    experts = lax.axis_size("node")
    groups = experts // GROUP_SIZE
    chosen_count = min(TOP_GROUPS, groups)
    capacity = tokens.shape[0] * chosen_count // groups
    placed, gating = slot_layout(routes, gate_codes, experts, capacity)
    place_low = placed.astype(jnp.bfloat16)
    weighted = placed * gating[:, :, None]
    gate_mat = w_gate[0]
    up_mat = w_up[0]
    down_mat = w_down[0]
    hidden_width = gate_mat.shape[1]

    def spread_tokens(payload):
        return jnp.einsum(
            "tep,tf->epf", place_low, payload, preferred_element_type=jnp.float32
        ).astype(jnp.bfloat16)

    def spread_cotangent(payload):
        return jnp.einsum(
            "tep,tf->epf", weighted, payload.astype(jnp.float32), precision=exact_mode
        ).astype(jnp.bfloat16)

    def project_in(totals, portion, offset):
        gate_next = jnp.einsum("epf,fh->eph", portion, gate_mat, preferred_element_type=jnp.float32)
        up_next = jnp.einsum("epf,fh->eph", portion, up_mat, preferred_element_type=jnp.float32)
        return (gate_next, up_next)

    empty_hidden = jnp.zeros((experts, capacity, hidden_width), jnp.float32)
    gate_pre, up_pre = deliver(tokens, spread_tokens, project_in, (empty_hidden, empty_hidden))
    squash = jax.nn.sigmoid(gate_pre)
    hidden = (gate_pre * squash * up_pre).astype(jnp.bfloat16)
    partial_value = jnp.einsum("eph,hf->epf", hidden, down_mat, preferred_element_type=jnp.float32)
    returned = send_back(partial_value)
    layer_out = jnp.einsum(
        "tep,epf->tf", weighted, returned.astype(jnp.float32), precision=exact_mode
    ).astype(jnp.bfloat16)

    def project_cotangent(totals, portion, offset):
        grad_next = jnp.einsum("epf,hf->eph", portion, down_mat, preferred_element_type=jnp.float32)
        block_grad = jnp.einsum("eph,epf->hf", hidden, portion, preferred_element_type=jnp.float32)
        return (grad_next, block_grad)

    empty_down = jnp.zeros((hidden_width, down_mat.shape[1]), jnp.float32)
    hidden_grad, down_total = deliver(
        cotangent, spread_cotangent, project_cotangent, (empty_hidden, empty_down)
    )
    gate_grad = (hidden_grad * up_pre * squash * (1.0 + gate_pre * (1.0 - squash))).astype(
        jnp.bfloat16
    )
    up_grad = (hidden_grad * gate_pre * squash).astype(jnp.bfloat16)
    partial_back = jnp.einsum(
        "eph,fh->epf", gate_grad, gate_mat, preferred_element_type=jnp.float32
    )
    partial_back = partial_back + jnp.einsum(
        "eph,fh->epf", up_grad, up_mat, preferred_element_type=jnp.float32
    )
    returned_back = send_back(partial_back)
    token_grad = jnp.einsum(
        "tep,epf->tf", placed, returned_back.astype(jnp.float32), precision=exact_mode
    ).astype(jnp.bfloat16)
    return (layer_out, token_grad, down_total.astype(jnp.bfloat16)[None])


def solution(mesh):
    in_specs = (
        P("node", "dev"),
        P("node", None),
        P("node", None),
        P("node", None, "dev"),
        P("node", None, "dev"),
        P("node", "dev", None),
        P("node", "dev"),
    )
    out_specs = (P("node", "dev"), P("node", "dev"), P("node", "dev", None))
    nodes, devs = mesh.shape["node"], mesh.shape["dev"]

    def body(tokens, routes, *rest):
        every = routes.shape[1] == nodes
        layer = fused if every and nodes == 8 and devs == 4 else on_device
        return layer(tokens, routes, *rest)

    return jax.shard_map(
        body, mesh=mesh, in_specs=in_specs, out_specs=out_specs, check_vma=False
    )
```

```python
import jax
import jax.numpy as jnp
from jax import lax
from jax.experimental import pallas as pl
from jax.experimental.pallas import tpu as pltpu
from jax.sharding import PartitionSpec as P

TOP_GROUPS = 4
GROUP_SIZE = 4
MESH_IDS = pl.DeviceIdType.MESH
ORDER_IN = (0, 1, 3, 2)
ORDER_OUT = (2, 1, 3, 0)
GROUP = 4


def dot(a, b, a_dim=1, b_dim=0):
    return lax.dot_general(
        a, b, (((a_dim,), (b_dim,)), ((), ())), preferred_element_type=jnp.float32
    )


def fused_kernel(
    pair_in, named_in, wg_in, wu_in, wd_in,
    layer_out, token_grad, down_out,
    x_all, gates, wg, wu, wd, gate_pre, up_pre, hid_grad, hidden, wcot, gate_grad, up_grad,
    part, r1, s1, r2, s2, r3, s3, r4, dgrad,
    in_send, in_recv, g_send, g_recv, out_send, out_recv, w_sem, own_sem, d_sem, named,
):
    node, d = lax.axis_index("node"), lax.axis_index("dev")
    y, x, c = node // 4, (node // 2) % 2, node % 2
    x_peer = (y * 2 + 1 - x) * 2 + c
    y_peer = ((1 - y) * 2 + x) * 2 + c
    c_peer = (y * 2 + x) * 2 + 1 - c
    width = pair_in.shape[2]
    rows = 8 * pair_in.shape[1]
    sent = []

    def send(src, dst, send_sem, recv_sem, target):
        copy = pltpu.make_async_remote_copy(
            src_ref=src, dst_ref=dst, send_sem=send_sem, recv_sem=recv_sem,
            device_id=target, device_id_type=MESH_IDS,
        )
        copy.start()
        sent.append(copy)
        return copy

    def column(k):
        return pl.ds(pl.multiple_of(((d + k) % 4) * width, width), width)

    barrier = pltpu.get_barrier_semaphore()
    peers = [(x_peer, d), (y_peer, d), (c_peer, d)] + [(node, (d + j) % 4) for j in (1, 2, 3)]
    for peer in peers:
        pl.semaphore_signal(barrier, inc=1, device_id=peer, device_id_type=MESH_IDS)

    own = [
        pltpu.make_async_copy(src, dst, own_sem.at[n])
        for n, (src, dst) in enumerate((
            (pair_in.at[0], x_all.at[0, 0, y, x, c]), (pair_in.at[1], x_all.at[1, 0, y, x, c]),
            (named_in, named),
        ))
    ]
    for copy in own:
        copy.start()

    loads = {}
    for k in ORDER_IN:
        loads["g", k] = pltpu.make_async_copy(wg_in.at[0, column(k)], wg.at[k], w_sem.at[0, k])
        loads["u", k] = pltpu.make_async_copy(wu_in.at[0, column(k)], wu.at[k], w_sem.at[1, k])
    for k in range(4):
        loads["d", k] = pltpu.make_async_copy(
            wd_in.at[0, :, column(k)], wd.at[k], w_sem.at[2, k]
        )
    for load in loads.values():
        load.start()
    for copy in own:
        copy.wait()

    here, choices = pair_in.shape[1], 8
    columns = named[...].T
    lane = lax.broadcasted_iota(jnp.int32, (here, 128), 1).astype(jnp.float32)
    table = jnp.zeros((here, 128), jnp.float32)
    for j in range(choices):
        weight = columns[:here, choices + j : choices + j + 1] / 65536.0
        table = table + jnp.where(columns[:here, j : j + 1] == lane, weight, 0.0)
    gates[y, x, c] = table


    pl.semaphore_wait(barrier, 6)

    z_hop = {}

    def start_z(a):
        own = x_all.at[a, 0, y, x, c]
        for j in (1, 3, 2):
            z_hop[a, 4 - j] = send(
                own, x_all.at[a, 4 - j, y, x, c], in_send.at[a, j, 0], in_recv.at[a, 4 - j, 0],
                (node, (d + j) % 4),
            )

    hop = {}

    def gather_stage(block, stage):
        a, i = divmod(block, 4)
        k = ORDER_IN[i]
        x_first = i % 2 == 0
        if stage == 0:
            if k:
                z_hop[a, k].wait_recv()
            ref = x_all.at[a, k, y, x, c]
            target = x_peer if x_first else y_peer
        else:
            hop[a, k].wait_recv()
            if stage == 1 and x_first:
                ref, target = x_all.at[a, k, y, :, c], y_peer
            elif stage == 1:
                ref, target = x_all.at[a, k, :, x, c], x_peer
            elif stage == 2:
                ref, target = x_all.at[a, k, :, :, c], c_peer
            else:
                return
        hop[a, k] = send(
            ref, ref, in_send.at[a, k, stage + 1], in_recv.at[a, k, stage + 1], (target, d)
        )

    def gates_stage(stage):
        if stage:
            hop["gates"].wait_recv()
        if stage < 3:
            ref, target = (
                (gates.at[y, x, c], x_peer),
                (gates.at[y, :, c], y_peer),
                (gates.at[:, :, c], c_peer),
            )[stage]
            hop["gates"] = send(ref, ref, g_send.at[stage], g_recv.at[stage], (target, d))

    def own_gates():
        table = gates[...].reshape(rows, 128)
        mine = lax.broadcasted_iota(jnp.int32, (rows, 128), 1) == node
        return jnp.sum(jnp.where(mine, table, 0.0), axis=1, keepdims=True)

    def project_in(i):
        k = ORDER_IN[i]
        lhs = x_all[0, k].reshape(rows, width)
        for name, weight, total in (("g", wg, gate_pre), ("u", wu, up_pre)):
            loads[name, k].wait()
            product = dot(lhs, weight[k])
            if i == 0:
                total[...] = product
            else:
                total[...] += product

    def make_hidden():
        pre = gate_pre[...]
        hidden[...] = (pre * jax.nn.sigmoid(pre) * up_pre[...]).astype(jnp.bfloat16)
        for k in range(4):
            loads["d", k].wait()

    def project_cotangent(i):
        k = ORDER_IN[i]
        values = x_all[1, k].reshape(rows, width).astype(jnp.float32)
        wcot[k] = (own_gates() * values).astype(jnp.bfloat16)
        product = dot(wcot[k], wd[k], 1, 1)
        if i == 0:
            hid_grad[...] = product
        else:
            hid_grad[...] += product

    def make_grads():
        pre, grad = gate_pre[...], hid_grad[...]
        q = jax.nn.sigmoid(pre)
        gate_grad[...] = (grad * up_pre[...] * q * (1.0 + pre * (1.0 - q))).astype(jnp.bfloat16)
        up_grad[...] = (grad * pre * q).astype(jnp.bfloat16)

    back = {}

    def add(one, other):
        return (one.astype(jnp.float32) + other.astype(jnp.float32)).astype(jnp.bfloat16)

    def return_stage(block, stage):
        b, i = divmod(block, 4)
        k = ORDER_OUT[i]
        x_first = i % 2 == 0
        if stage == 0:
            if b == 0:
                value = own_gates() * dot(hidden[...], wd[k])
            else:
                value = dot(gate_grad[...], wg[k], 1, 1) + dot(up_grad[...], wu[k], 1, 1)
            part[b, k] = value.astype(jnp.bfloat16).reshape(part.shape[2:])
            src, dst, target = part.at[b, k, :, :, 1 - c], r1.at[b, k], c_peer
        elif stage == 1:
            back[b, k].wait_recv()
            s1[b, k] = add(part[b, k, :, :, c], r1[b, k])
            if x_first:
                src, target = s1.at[b, k, :, 1 - x], x_peer
            else:
                src, target = s1.at[b, k, 1 - y], y_peer
            dst = r2.at[b, k]
        elif stage == 2:
            back[b, k].wait_recv()
            s2[b, k] = add(s1[b, k, :, x] if x_first else s1[b, k, y], r2[b, k])
            if x_first:
                src, target = s2.at[b, k, 1 - y], y_peer
            else:
                src, target = s2.at[b, k, 1 - x], x_peer
            dst = r3.at[b, k]
        else:
            back[b, k].wait_recv()
            s3[b, k] = add(s2[b, k, y] if x_first else s2[b, k, x], r3[b, k])
            if k:
                back[b, "z", 4 - k] = send(
                    s3.at[b, k], r4.at[b, 4 - k], out_send.at[b, k, 3], out_recv.at[b, 4 - k, 3],
                    (node, (d + k) % 4),
                )
            return
        back[b, k] = send(
            src, dst, out_send.at[b, k, stage], out_recv.at[b, k, stage], (target, d)
        )

    def finish(b, result):
        total = s3[b, 0].astype(jnp.float32)
        for k in (1, 3, 2):
            back[b, "z", k].wait_recv()
            total = total + r4[b, k].astype(jnp.float32)
        result[...] = total.astype(jnp.bfloat16)

    stores = []

    def down_block(k):
        dgrad[k] = dot(hidden[...], wcot[k], 0, 0).astype(jnp.bfloat16)
        store = pltpu.make_async_copy(dgrad.at[k], down_out.at[0, :, column(k)], d_sem.at[k])
        store.start()
        stores.append(store)

    start_z(0)
    gates_stage(0)
    groups = 8 // GROUP
    ready = groups // 2 + 2
    last = ready + groups + 3

    def members(group):
        return range(group * GROUP, group * GROUP + GROUP) if 0 <= group < groups else ()

    for slot in range(last):
        for stage in (3, 2, 1, 0):
            for block in members(slot - stage):
                gather_stage(block, stage)
        if slot == 0:
            start_z(1)
        if 1 <= slot <= 3:
            gates_stage(slot)
        for block in members(slot - 3):
            if block < 4:
                project_in(block)
        if slot == ready:
            make_hidden()
        for block in members(slot - ready):
            if block < 4:
                return_stage(block, 0)
        for block in members(slot - 3):
            if block >= 4:
                project_cotangent(block - 4)
        if slot == groups + 2:
            make_grads()
        for block in members(slot - ready):
            if block >= 4:
                return_stage(block, 0)
        if slot >= last - 3:
            for k in ((0, 1), (2,), (3,))[slot - (last - 3)]:
                down_block(k)
        for stage in (3, 2, 1):
            for block in members(slot - ready - stage):
                return_stage(block, stage)
    finish(0, layer_out)
    finish(1, token_grad)
    for copy in sent:
        copy.wait_send()
    for store in stores:
        store.wait()


def fused(tokens, routes, gate_codes, w_gate, w_up, w_down, cotangent):
    here, width = tokens.shape
    hidden_width = w_gate.shape[2]
    rows = 8 * here
    low, full = jnp.bfloat16, jnp.float32
    vmem = pl.BlockSpec(memory_space=pltpu.VMEM)
    anywhere = pl.BlockSpec(memory_space=pl.ANY)
    dma = pltpu.SemaphoreType.DMA
    scratch = [
        pltpu.VMEM((2, 4, 2, 2, 2, here, width), low),
        pltpu.VMEM((2, 2, 2, here, 128), full),
        pltpu.VMEM((4, width, hidden_width), low),
        pltpu.VMEM((4, width, hidden_width), low),
        pltpu.VMEM((4, hidden_width, width), low),
        pltpu.VMEM((rows, hidden_width), full),
        pltpu.VMEM((rows, hidden_width), full),
        pltpu.VMEM((rows, hidden_width), full),
        pltpu.VMEM((rows, hidden_width), low),
        pltpu.VMEM((4, rows, width), low),
        pltpu.VMEM((rows, hidden_width), low),
        pltpu.VMEM((rows, hidden_width), low),
        pltpu.VMEM((2, 4, 2, 2, 2, here, width), low),
        pltpu.VMEM((2, 4, 2, 2, here, width), low),
        pltpu.VMEM((2, 4, 2, 2, here, width), low),
        pltpu.VMEM((2, 4, 2, here, width), low),
        pltpu.VMEM((2, 4, 2, here, width), low),
        pltpu.VMEM((2, 4, here, width), low),
        pltpu.VMEM((2, 4, here, width), low),
        pltpu.VMEM((2, 4, here, width), low),
        pltpu.VMEM((4, hidden_width, width), low),
        dma((2, 4, 4)), dma((2, 4, 4)), dma((3,)), dma((3,)), dma((2, 4, 4)), dma((2, 4, 4)),
        dma((3, 4)), dma((3,)), dma((4,)),
        pltpu.VMEM((128, 128), full),
    ]
    named = jnp.concatenate([routes.T, gate_codes.T], axis=0).astype(full)
    named = jnp.pad(named, ((0, 128 - named.shape[0]), (0, 128 - here)))
    flops = 2 * 7 * rows * 4 * width * hidden_width
    return pl.pallas_call(
        fused_kernel,
        out_shape=(
            jax.ShapeDtypeStruct(tokens.shape, low),
            jax.ShapeDtypeStruct(tokens.shape, low),
            jax.ShapeDtypeStruct(w_down.shape, low),
        ),
        in_specs=[anywhere] * 5,
        out_specs=(vmem, vmem, anywhere),
        scratch_shapes=scratch,
        compiler_params=pltpu.CompilerParams(
            collective_id=0, has_side_effects=True, vmem_limit_bytes=48 * 1024 * 1024
        ),
        cost_estimate=pl.CostEstimate(
            flops=flops, bytes_accessed=8 * w_gate.size, transcendentals=2 * rows * hidden_width
        ),
    )(jnp.stack([tokens, cotangent]), named, w_gate, w_up, w_down)


exact_mode = lax.Precision.HIGHEST


def slot_layout(routes, gate_codes, experts, capacity):
    tokens_here = routes.shape[0]
    member = (routes[:, :, None] == jnp.arange(experts, dtype=jnp.int32)[None, None, :]).astype(
        jnp.float32
    )
    named_by = jnp.sum(member, axis=1)
    earlier = (jnp.arange(tokens_here)[:, None] > jnp.arange(tokens_here)[None, :]).astype(
        jnp.float32
    )
    before = jnp.dot(earlier, named_by, precision=exact_mode)
    placed = named_by[:, :, None] * (
        before[:, :, None] == jnp.arange(capacity).astype(jnp.float32)[None, None, :]
    ).astype(jnp.float32)
    weights = gate_codes.astype(jnp.float32) / 65536.0
    gating = jnp.sum(member * weights[:, :, None], axis=1)
    return (placed, gating)


def deliver(local_rows, build, fold, initial):
    whole_rows = lax.all_gather(local_rows, "dev", axis=1, tiled=True)
    arrived = lax.all_to_all(build(whole_rows), "node", split_axis=0, concat_axis=0, tiled=True)
    return fold(initial, arrived, 0)


def send_back(partial_value):
    shares = lax.psum_scatter(
        partial_value.astype(jnp.bfloat16), "dev", scatter_dimension=2, tiled=True
    )
    return lax.all_to_all(shares, "node", split_axis=0, concat_axis=0, tiled=True)


def on_device(tokens, routes, gate_codes, w_gate, w_up, w_down, cotangent):
    experts = lax.axis_size("node")
    groups = experts // GROUP_SIZE
    chosen_count = min(TOP_GROUPS, groups)
    capacity = tokens.shape[0] * chosen_count // groups
    placed, gating = slot_layout(routes, gate_codes, experts, capacity)
    place_low = placed.astype(jnp.bfloat16)
    weighted = placed * gating[:, :, None]
    gate_mat = w_gate[0]
    up_mat = w_up[0]
    down_mat = w_down[0]
    hidden_width = gate_mat.shape[1]

    def spread_tokens(payload):
        return jnp.einsum(
            "tep,tf->epf", place_low, payload, preferred_element_type=jnp.float32
        ).astype(jnp.bfloat16)

    def spread_cotangent(payload):
        return jnp.einsum(
            "tep,tf->epf", weighted, payload.astype(jnp.float32), precision=exact_mode
        ).astype(jnp.bfloat16)

    def project_in(totals, portion, offset):
        gate_next = jnp.einsum("epf,fh->eph", portion, gate_mat, preferred_element_type=jnp.float32)
        up_next = jnp.einsum("epf,fh->eph", portion, up_mat, preferred_element_type=jnp.float32)
        return (gate_next, up_next)

    empty_hidden = jnp.zeros((experts, capacity, hidden_width), jnp.float32)
    gate_pre, up_pre = deliver(tokens, spread_tokens, project_in, (empty_hidden, empty_hidden))
    squash = jax.nn.sigmoid(gate_pre)
    hidden = (gate_pre * squash * up_pre).astype(jnp.bfloat16)
    partial_value = jnp.einsum("eph,hf->epf", hidden, down_mat, preferred_element_type=jnp.float32)
    returned = send_back(partial_value)
    layer_out = jnp.einsum(
        "tep,epf->tf", weighted, returned.astype(jnp.float32), precision=exact_mode
    ).astype(jnp.bfloat16)

    def project_cotangent(totals, portion, offset):
        grad_next = jnp.einsum("epf,hf->eph", portion, down_mat, preferred_element_type=jnp.float32)
        block_grad = jnp.einsum("eph,epf->hf", hidden, portion, preferred_element_type=jnp.float32)
        return (grad_next, block_grad)

    empty_down = jnp.zeros((hidden_width, down_mat.shape[1]), jnp.float32)
    hidden_grad, down_total = deliver(
        cotangent, spread_cotangent, project_cotangent, (empty_hidden, empty_down)
    )
    gate_grad = (hidden_grad * up_pre * squash * (1.0 + gate_pre * (1.0 - squash))).astype(
        jnp.bfloat16
    )
    up_grad = (hidden_grad * gate_pre * squash).astype(jnp.bfloat16)
    partial_back = jnp.einsum(
        "eph,fh->epf", gate_grad, gate_mat, preferred_element_type=jnp.float32
    )
    partial_back = partial_back + jnp.einsum(
        "eph,fh->epf", up_grad, up_mat, preferred_element_type=jnp.float32
    )
    returned_back = send_back(partial_back)
    token_grad = jnp.einsum(
        "tep,epf->tf", placed, returned_back.astype(jnp.float32), precision=exact_mode
    ).astype(jnp.bfloat16)
    return (layer_out, token_grad, down_total.astype(jnp.bfloat16)[None])


def solution(mesh):
    in_specs = (
        P("node", "dev"),
        P("node", None),
        P("node", None),
        P("node", None, "dev"),
        P("node", None, "dev"),
        P("node", "dev", None),
        P("node", "dev"),
    )
    out_specs = (P("node", "dev"), P("node", "dev"), P("node", "dev", None))
    nodes, devs = mesh.shape["node"], mesh.shape["dev"]

    def body(tokens, routes, *rest):
        every = routes.shape[1] == nodes
        layer = fused if every and nodes == 8 and devs == 4 else on_device
        return layer(tokens, routes, *rest)

    return jax.shard_map(
        body, mesh=mesh, in_specs=in_specs, out_specs=out_specs, check_vma=False
    )
```

```python
import jax
import jax.numpy as jnp
from jax import lax
from jax.experimental import pallas as pl
from jax.experimental.pallas import tpu as pltpu
from jax.sharding import PartitionSpec as P

TOP_GROUPS = 4
GROUP_SIZE = 4
MESH_IDS = pl.DeviceIdType.MESH
ORDER_IN = (0, 1, 3, 2)
ORDER_OUT = (2, 1, 3, 0)
GROUP = 4


def dot(a, b, a_dim=1, b_dim=0):
    return lax.dot_general(
        a, b, (((a_dim,), (b_dim,)), ((), ())), preferred_element_type=jnp.float32
    )


def fused_kernel(
    pair_in, named_in, wg_in, wu_in, wd_in,
    layer_out, token_grad, down_out,
    x_all, gates, wg, wu, wd, gate_pre, up_pre, hid_grad, hidden, wcot, gate_grad, up_grad,
    part, r1, s1, r2, s2, r3, s3, r4, dgrad,
    in_send, in_recv, g_send, g_recv, out_send, out_recv, w_sem, own_sem, d_sem, named,
):
    node, d = lax.axis_index("node"), lax.axis_index("dev")
    y, x, c = node // 4, (node // 2) % 2, node % 2
    x_peer = (y * 2 + 1 - x) * 2 + c
    y_peer = ((1 - y) * 2 + x) * 2 + c
    c_peer = (y * 2 + x) * 2 + 1 - c
    width = pair_in.shape[2]
    rows = 8 * pair_in.shape[1]
    sent = []

    def send(src, dst, send_sem, recv_sem, target):
        copy = pltpu.make_async_remote_copy(
            src_ref=src, dst_ref=dst, send_sem=send_sem, recv_sem=recv_sem,
            device_id=target, device_id_type=MESH_IDS,
        )
        copy.start()
        sent.append(copy)
        return copy

    def column(k):
        return pl.ds(pl.multiple_of(((d + k) % 4) * width, width), width)

    barrier = pltpu.get_barrier_semaphore()
    peers = [(x_peer, d), (y_peer, d), (c_peer, d)] + [(node, (d + j) % 4) for j in (1, 2, 3)]
    for peer in peers:
        pl.semaphore_signal(barrier, inc=1, device_id=peer, device_id_type=MESH_IDS)

    own = [
        pltpu.make_async_copy(src, dst, own_sem.at[n])
        for n, (src, dst) in enumerate((
            (pair_in.at[0], x_all.at[0, 0, y, x, c]), (pair_in.at[1], x_all.at[1, 0, y, x, c]),
            (named_in, named),
        ))
    ]
    for copy in own:
        copy.start()

    loads = {}
    for k in ORDER_IN:
        loads["g", k] = pltpu.make_async_copy(wg_in.at[0, column(k)], wg.at[k], w_sem.at[0, k])
        loads["u", k] = pltpu.make_async_copy(wu_in.at[0, column(k)], wu.at[k], w_sem.at[1, k])
    for k in range(4):
        loads["d", k] = pltpu.make_async_copy(
            wd_in.at[0, :, column(k)], wd.at[k], w_sem.at[2, k]
        )
    for load in loads.values():
        load.start()
    for copy in own:
        copy.wait()

    here, choices = pair_in.shape[1], 8
    columns = named[...].T
    lane = lax.broadcasted_iota(jnp.int32, (here, 128), 1).astype(jnp.float32)
    table = jnp.zeros((here, 128), jnp.float32)
    for j in range(choices):
        weight = columns[:here, choices + j : choices + j + 1] / 65536.0
        table = table + jnp.where(columns[:here, j : j + 1] == lane, weight, 0.0)
    gates[y, x, c] = table


    pl.semaphore_wait(barrier, 6)

    z_hop = {}

    def start_z(a):
        own = x_all.at[a, 0, y, x, c]
        for j in (1, 3, 2):
            z_hop[a, 4 - j] = send(
                own, x_all.at[a, 4 - j, y, x, c], in_send.at[a, j, 0], in_recv.at[a, 4 - j, 0],
                (node, (d + j) % 4),
            )

    hop = {}

    def gather_stage(block, stage):
        a, i = divmod(block, 4)
        k = ORDER_IN[i]
        x_first = i % 2 == 0
        if stage == 0:
            if k:
                z_hop[a, k].wait_recv()
            ref = x_all.at[a, k, y, x, c]
            target = x_peer if x_first else y_peer
        else:
            hop[a, k].wait_recv()
            if stage == 1 and x_first:
                ref, target = x_all.at[a, k, y, :, c], y_peer
            elif stage == 1:
                ref, target = x_all.at[a, k, :, x, c], x_peer
            elif stage == 2:
                ref, target = x_all.at[a, k, :, :, c], c_peer
            else:
                return
        hop[a, k] = send(
            ref, ref, in_send.at[a, k, stage + 1], in_recv.at[a, k, stage + 1], (target, d)
        )

    def gates_stage(stage):
        if stage:
            hop["gates"].wait_recv()
        if stage < 3:
            ref, target = (
                (gates.at[y, x, c], x_peer),
                (gates.at[y, :, c], y_peer),
                (gates.at[:, :, c], c_peer),
            )[stage]
            hop["gates"] = send(ref, ref, g_send.at[stage], g_recv.at[stage], (target, d))

    def own_gates():
        table = gates[...].reshape(rows, 128)
        mine = lax.broadcasted_iota(jnp.int32, (rows, 128), 1) == node
        return jnp.sum(jnp.where(mine, table, 0.0), axis=1, keepdims=True)

    def project_in(i):
        k = ORDER_IN[i]
        lhs = x_all[0, k].reshape(rows, width)
        for name, weight, total in (("g", wg, gate_pre), ("u", wu, up_pre)):
            loads[name, k].wait()
            product = dot(lhs, weight[k])
            if i == 0:
                total[...] = product
            else:
                total[...] += product

    def make_hidden():
        pre = gate_pre[...]
        hidden[...] = (pre * jax.nn.sigmoid(pre) * up_pre[...]).astype(jnp.bfloat16)
        for k in range(4):
            loads["d", k].wait()

    def project_cotangent(i):
        k = ORDER_IN[i]
        values = x_all[1, k].reshape(rows, width).astype(jnp.float32)
        wcot[k] = (own_gates() * values).astype(jnp.bfloat16)
        product = dot(wcot[k], wd[k], 1, 1)
        if i == 0:
            hid_grad[...] = product
        else:
            hid_grad[...] += product

    def make_grads():
        pre, grad = gate_pre[...], hid_grad[...]
        q = jax.nn.sigmoid(pre)
        gate_grad[...] = (grad * up_pre[...] * q * (1.0 + pre * (1.0 - q))).astype(jnp.bfloat16)
        up_grad[...] = (grad * pre * q).astype(jnp.bfloat16)

    back = {}

    def add(one, other):
        return (one.astype(jnp.float32) + other.astype(jnp.float32)).astype(jnp.bfloat16)

    def return_stage(block, stage):
        b, i = divmod(block, 4)
        k = ORDER_OUT[i]
        x_first = i % 2 == 0
        if stage == 0:
            if b == 0:
                value = own_gates() * dot(hidden[...], wd[k])
            else:
                value = dot(gate_grad[...], wg[k], 1, 1) + dot(up_grad[...], wu[k], 1, 1)
            part[b, k] = value.astype(jnp.bfloat16).reshape(part.shape[2:])
            src, dst, target = part.at[b, k, :, :, 1 - c], r1.at[b, k], c_peer
        elif stage == 1:
            back[b, k].wait_recv()
            s1[b, k] = add(part[b, k, :, :, c], r1[b, k])
            if x_first:
                src, target = s1.at[b, k, :, 1 - x], x_peer
            else:
                src, target = s1.at[b, k, 1 - y], y_peer
            dst = r2.at[b, k]
        elif stage == 2:
            back[b, k].wait_recv()
            s2[b, k] = add(s1[b, k, :, x] if x_first else s1[b, k, y], r2[b, k])
            if x_first:
                src, target = s2.at[b, k, 1 - y], y_peer
            else:
                src, target = s2.at[b, k, 1 - x], x_peer
            dst = r3.at[b, k]
        else:
            back[b, k].wait_recv()
            s3[b, k] = add(s2[b, k, y] if x_first else s2[b, k, x], r3[b, k])
            if k:
                back[b, "z", 4 - k] = send(
                    s3.at[b, k], r4.at[b, 4 - k], out_send.at[b, k, 3], out_recv.at[b, 4 - k, 3],
                    (node, (d + k) % 4),
                )
            return
        back[b, k] = send(
            src, dst, out_send.at[b, k, stage], out_recv.at[b, k, stage], (target, d)
        )

    def finish(b, result):
        total = s3[b, 0].astype(jnp.float32)
        for k in (1, 3, 2):
            back[b, "z", k].wait_recv()
            total = total + r4[b, k].astype(jnp.float32)
        result[...] = total.astype(jnp.bfloat16)

    stores = []

    def down_block(k):
        dgrad[k] = dot(hidden[...], wcot[k], 0, 0).astype(jnp.bfloat16)
        store = pltpu.make_async_copy(dgrad.at[k], down_out.at[0, :, column(k)], d_sem.at[k])
        store.start()
        stores.append(store)

    start_z(0)
    gates_stage(0)
    groups = 8 // GROUP
    ready = groups // 2 + 2
    last = ready + groups + 3

    def members(group):
        return range(group * GROUP, group * GROUP + GROUP) if 0 <= group < groups else ()

    for slot in range(last):
        for stage in (3, 2, 1, 0):
            for block in members(slot - stage):
                gather_stage(block, stage)
        if slot == 0:
            start_z(1)
        if 1 <= slot <= 3:
            gates_stage(slot)
        for block in members(slot - 3):
            if block < 4:
                project_in(block)
        if slot == ready:
            make_hidden()
        for block in members(slot - ready):
            if block < 4:
                return_stage(block, 0)
        for block in members(slot - 3):
            if block >= 4:
                project_cotangent(block - 4)
        if slot == groups + 2:
            make_grads()
        early = slot == ready + 1
        for block in range(4 if early else 0):
            return_stage(block, 1)
        for block in members(slot - ready):
            if block >= 4:
                return_stage(block, 0)
        for block in range(4 if early else 0):
            return_stage(block, 2)
        if slot >= last - 3:
            for k in ((0, 1), (2,), (3,))[slot - (last - 3)]:
                down_block(k)
        for stage in (3, 2, 1):
            for block in members(slot - ready - stage):
                if block >= 4:
                    return_stage(block, stage)
        if slot == last - 2:
            for block in range(4):
                return_stage(block, 3)
    finish(0, layer_out)
    finish(1, token_grad)
    for copy in sent:
        copy.wait_send()
    for store in stores:
        store.wait()


def fused(tokens, routes, gate_codes, w_gate, w_up, w_down, cotangent):
    here, width = tokens.shape
    hidden_width = w_gate.shape[2]
    rows = 8 * here
    low, full = jnp.bfloat16, jnp.float32
    vmem = pl.BlockSpec(memory_space=pltpu.VMEM)
    anywhere = pl.BlockSpec(memory_space=pl.ANY)
    dma = pltpu.SemaphoreType.DMA
    scratch = [
        pltpu.VMEM((2, 4, 2, 2, 2, here, width), low),
        pltpu.VMEM((2, 2, 2, here, 128), full),
        pltpu.VMEM((4, width, hidden_width), low),
        pltpu.VMEM((4, width, hidden_width), low),
        pltpu.VMEM((4, hidden_width, width), low),
        pltpu.VMEM((rows, hidden_width), full),
        pltpu.VMEM((rows, hidden_width), full),
        pltpu.VMEM((rows, hidden_width), full),
        pltpu.VMEM((rows, hidden_width), low),
        pltpu.VMEM((4, rows, width), low),
        pltpu.VMEM((rows, hidden_width), low),
        pltpu.VMEM((rows, hidden_width), low),
        pltpu.VMEM((2, 4, 2, 2, 2, here, width), low),
        pltpu.VMEM((2, 4, 2, 2, here, width), low),
        pltpu.VMEM((2, 4, 2, 2, here, width), low),
        pltpu.VMEM((2, 4, 2, here, width), low),
        pltpu.VMEM((2, 4, 2, here, width), low),
        pltpu.VMEM((2, 4, here, width), low),
        pltpu.VMEM((2, 4, here, width), low),
        pltpu.VMEM((2, 4, here, width), low),
        pltpu.VMEM((4, hidden_width, width), low),
        dma((2, 4, 4)), dma((2, 4, 4)), dma((3,)), dma((3,)), dma((2, 4, 4)), dma((2, 4, 4)),
        dma((3, 4)), dma((3,)), dma((4,)),
        pltpu.VMEM((128, 128), full),
    ]
    named = jnp.concatenate([routes.T, gate_codes.T], axis=0).astype(full)
    named = jnp.pad(named, ((0, 128 - named.shape[0]), (0, 128 - here)))
    flops = 2 * 7 * rows * 4 * width * hidden_width
    return pl.pallas_call(
        fused_kernel,
        out_shape=(
            jax.ShapeDtypeStruct(tokens.shape, low),
            jax.ShapeDtypeStruct(tokens.shape, low),
            jax.ShapeDtypeStruct(w_down.shape, low),
        ),
        in_specs=[anywhere] * 5,
        out_specs=(vmem, vmem, anywhere),
        scratch_shapes=scratch,
        compiler_params=pltpu.CompilerParams(
            collective_id=0, has_side_effects=True, vmem_limit_bytes=48 * 1024 * 1024
        ),
        cost_estimate=pl.CostEstimate(
            flops=flops, bytes_accessed=8 * w_gate.size, transcendentals=2 * rows * hidden_width
        ),
    )(jnp.stack([tokens, cotangent]), named, w_gate, w_up, w_down)


exact_mode = lax.Precision.HIGHEST


def slot_layout(routes, gate_codes, experts, capacity):
    tokens_here = routes.shape[0]
    member = (routes[:, :, None] == jnp.arange(experts, dtype=jnp.int32)[None, None, :]).astype(
        jnp.float32
    )
    named_by = jnp.sum(member, axis=1)
    earlier = (jnp.arange(tokens_here)[:, None] > jnp.arange(tokens_here)[None, :]).astype(
        jnp.float32
    )
    before = jnp.dot(earlier, named_by, precision=exact_mode)
    placed = named_by[:, :, None] * (
        before[:, :, None] == jnp.arange(capacity).astype(jnp.float32)[None, None, :]
    ).astype(jnp.float32)
    weights = gate_codes.astype(jnp.float32) / 65536.0
    gating = jnp.sum(member * weights[:, :, None], axis=1)
    return (placed, gating)


def deliver(local_rows, build, fold, initial):
    whole_rows = lax.all_gather(local_rows, "dev", axis=1, tiled=True)
    arrived = lax.all_to_all(build(whole_rows), "node", split_axis=0, concat_axis=0, tiled=True)
    return fold(initial, arrived, 0)


def send_back(partial_value):
    shares = lax.psum_scatter(
        partial_value.astype(jnp.bfloat16), "dev", scatter_dimension=2, tiled=True
    )
    return lax.all_to_all(shares, "node", split_axis=0, concat_axis=0, tiled=True)


def on_device(tokens, routes, gate_codes, w_gate, w_up, w_down, cotangent):
    experts = lax.axis_size("node")
    groups = experts // GROUP_SIZE
    chosen_count = min(TOP_GROUPS, groups)
    capacity = tokens.shape[0] * chosen_count // groups
    placed, gating = slot_layout(routes, gate_codes, experts, capacity)
    place_low = placed.astype(jnp.bfloat16)
    weighted = placed * gating[:, :, None]
    gate_mat = w_gate[0]
    up_mat = w_up[0]
    down_mat = w_down[0]
    hidden_width = gate_mat.shape[1]

    def spread_tokens(payload):
        return jnp.einsum(
            "tep,tf->epf", place_low, payload, preferred_element_type=jnp.float32
        ).astype(jnp.bfloat16)

    def spread_cotangent(payload):
        return jnp.einsum(
            "tep,tf->epf", weighted, payload.astype(jnp.float32), precision=exact_mode
        ).astype(jnp.bfloat16)

    def project_in(totals, portion, offset):
        gate_next = jnp.einsum("epf,fh->eph", portion, gate_mat, preferred_element_type=jnp.float32)
        up_next = jnp.einsum("epf,fh->eph", portion, up_mat, preferred_element_type=jnp.float32)
        return (gate_next, up_next)

    empty_hidden = jnp.zeros((experts, capacity, hidden_width), jnp.float32)
    gate_pre, up_pre = deliver(tokens, spread_tokens, project_in, (empty_hidden, empty_hidden))
    squash = jax.nn.sigmoid(gate_pre)
    hidden = (gate_pre * squash * up_pre).astype(jnp.bfloat16)
    partial_value = jnp.einsum("eph,hf->epf", hidden, down_mat, preferred_element_type=jnp.float32)
    returned = send_back(partial_value)
    layer_out = jnp.einsum(
        "tep,epf->tf", weighted, returned.astype(jnp.float32), precision=exact_mode
    ).astype(jnp.bfloat16)

    def project_cotangent(totals, portion, offset):
        grad_next = jnp.einsum("epf,hf->eph", portion, down_mat, preferred_element_type=jnp.float32)
        block_grad = jnp.einsum("eph,epf->hf", hidden, portion, preferred_element_type=jnp.float32)
        return (grad_next, block_grad)

    empty_down = jnp.zeros((hidden_width, down_mat.shape[1]), jnp.float32)
    hidden_grad, down_total = deliver(
        cotangent, spread_cotangent, project_cotangent, (empty_hidden, empty_down)
    )
    gate_grad = (hidden_grad * up_pre * squash * (1.0 + gate_pre * (1.0 - squash))).astype(
        jnp.bfloat16
    )
    up_grad = (hidden_grad * gate_pre * squash).astype(jnp.bfloat16)
    partial_back = jnp.einsum(
        "eph,fh->epf", gate_grad, gate_mat, preferred_element_type=jnp.float32
    )
    partial_back = partial_back + jnp.einsum(
        "eph,fh->epf", up_grad, up_mat, preferred_element_type=jnp.float32
    )
    returned_back = send_back(partial_back)
    token_grad = jnp.einsum(
        "tep,epf->tf", placed, returned_back.astype(jnp.float32), precision=exact_mode
    ).astype(jnp.bfloat16)
    return (layer_out, token_grad, down_total.astype(jnp.bfloat16)[None])


def solution(mesh):
    in_specs = (
        P("node", "dev"),
        P("node", None),
        P("node", None),
        P("node", None, "dev"),
        P("node", None, "dev"),
        P("node", "dev", None),
        P("node", "dev"),
    )
    out_specs = (P("node", "dev"), P("node", "dev"), P("node", "dev", None))
    nodes, devs = mesh.shape["node"], mesh.shape["dev"]

    def body(tokens, routes, *rest):
        every = routes.shape[1] == nodes
        layer = fused if every and nodes == 8 and devs == 4 else on_device
        return layer(tokens, routes, *rest)

    return jax.shard_map(
        body, mesh=mesh, in_specs=in_specs, out_specs=out_specs, check_vma=False
    )
```
